512 devices in a mesh: gx: 16 (over x, z_lo), gy: 32 (over z_hi, y, core).
Axes of the slice: x: 4, y: 4, z: 16 (z_hi: 4, z_lo: 4; z = z_hi * 4 + z_lo), core: 2. Of those that a mesh axis runs over, the one named last changes fastest.
Arguments:
- object_slices: float32 [4, 2, 2048, 4096], P(None, None, 'gy', 'gx'), may hold values from -6 to 6
- probe: float32 [2, 128, 128], replicated, may hold values from -6 to 6
- positions: int32 [32, 16, 2, 2], P('gy', 'gx'), may hold values from 0 to 3968, as said below
- counts: int32 [32, 16], P('gy', 'gx'), may hold values from 1 to 2, as said below
- measured: float32 [32, 16, 2, 128, 128], P('gy', 'gx'), may hold values from 0.05 to 1
Outputs:
- object_grad: float32 [4, 2, 2048, 4096], P(None, None, 'gy', 'gx')
- probe_grad: float32 [2, 128, 128], replicated
The draws below stay inside these ranges and needn't reach their ends.
Inputs may be any that keep to these rules, and one draw needn't show every extreme that they name: `positions`: slot k of tile (ty, tx) has its corner at row ty * 64 + a and column tx * 256 + b with a between -64 and 0 and b between -64 and 192, moved inward where needed so that the whole patch lies inside the region. `counts`: slots at or above a tile's count are not used.
All inputs are finite; a program needn't handle non-finite values.
Results may differ from the reference program's by a relative error of at most 0.0003.
Values sent between devices are 32-bit elements; how exact they have to be, the bound alone decides.
No kernel may reach another device: no remote copies, remote signals or barrier semaphores. Data moves between devices by JAX's collectives and lax.ppermute only.
A program may use at most 64 MiB of HBM per device.

```python
import math
import jax
import jax.numpy as jnp
from jax import lax

PROBE_PATCH_SIDE = 128
SLICES = 4
TR = 64
TC = 256
P_MAX = 2
ROWS = 2048
COLS = 4096
N_GX = 16
N_GY = 32


def draw_positions(key, part):
    key = jax.random.fold_in(key, 11)
    half_patch = PROBE_PATCH_SIDE // 2
    row_key, col_key = jax.random.split(key)
    row_offset = jax.random.randint(row_key, (N_GY, N_GX, P_MAX), -half_patch, TR - half_patch + 1)
    col_offset = jax.random.randint(col_key, (N_GY, N_GX, P_MAX), -half_patch, TC - half_patch + 1)
    row_offset = row_offset.at[0, 0, 0].set(-half_patch).at[N_GY - 1, N_GX - 1, 0].set(TR - half_patch)
    col_offset = col_offset.at[0, 0, 0].set(-half_patch).at[N_GY - 1, N_GX - 1, 0].set(TC - half_patch)
    row_corner = jnp.arange(N_GY)[:, None, None] * TR + row_offset
    col_corner = jnp.arange(N_GX)[None, :, None] * TC + col_offset
    row_corner = jnp.clip(row_corner, 0, TR * N_GY - PROBE_PATCH_SIDE)
    col_corner = jnp.clip(col_corner, 0, TC * N_GX - PROBE_PATCH_SIDE)
    return jnp.stack([row_corner, col_corner], axis=-1).astype(jnp.int32)


def draw_counts(key, part):
    key = jax.random.fold_in(key, 12)
    first_key, second_key, third_key = jax.random.split(key, 3)
    low_draw = jax.random.randint(first_key, (N_GY, N_GX), 1, P_MAX + 1)
    high_draw = jax.random.randint(second_key, (N_GY, N_GX), 1, P_MAX + 1)
    tile_counts = jnp.minimum(low_draw, high_draw).reshape(-1)
    busiest = jax.random.randint(third_key, (), 0, N_GY * N_GX)
    tile_counts = tile_counts.at[busiest].set(P_MAX)
    tile_counts = tile_counts.at[(busiest + 1) % (N_GY * N_GX)].set(1)
    return tile_counts.reshape(N_GY, N_GX).astype(jnp.int32)


def steps_of(stream_key, shape, shards, low, high):
    gain, own = 1.0, jax.random.fold_in(stream_key, 6)
    for dim, shards_of in shards:
        steps = jnp.exp(jax.random.uniform(jax.random.fold_in(own, dim), (shards_of,), jnp.float32, low / len(shards), high / len(shards)))
        gain = gain * jnp.repeat(steps, shape[dim] // shards_of).reshape([-1 if axis == dim else 1 for axis in range(len(shape))])
    return gain


def scatter_about(key, dims, spread, bound, cuts=(), kind=jnp.bfloat16):
    values = spread * jax.random.normal(key, dims, jnp.float32)
    if cuts:
        values = values * steps_of(key, dims, cuts, -0.22, 0.18)
    return jnp.clip(values, -bound, bound).astype(kind)


def setup_inputs(seed: int = 0) -> dict:
    splits = jax.random.split(jax.random.key(seed), 6)
    object_slices = scatter_about(splits[0], (SLICES, 2, ROWS, COLS), 0.7071, 6.0, ((2, 32), (3, 16)), jnp.float32)
    probe = scatter_about(splits[1], (2, PROBE_PATCH_SIDE, PROBE_PATCH_SIDE), 1.0, 6.0, (), jnp.float32)
    positions = draw_positions(jax.random.fold_in(splits[5], 71), 0)
    counts = draw_counts(jax.random.fold_in(splits[5], 71), 0)
    measured = jnp.clip(jnp.exp(math.log(1.0) - 2.9957323 * jax.random.uniform(splits[4], (N_GY, N_GX, P_MAX, PROBE_PATCH_SIDE, PROBE_PATCH_SIDE), jnp.float32) ** steps_of(splits[4], (N_GY, N_GX, P_MAX, PROBE_PATCH_SIDE, PROBE_PATCH_SIDE), ((0, 32), (1, 16)), -0.2, 0.2)), 0.05, 1.0)
    return {"object_slices": object_slices, "probe": probe, "positions": positions, "counts": counts, "measured": measured}


distance = 0.5


def kernel_phase(patch_size):
    indices = jnp.arange(patch_size)
    frequency = ((indices + patch_size // 2) % patch_size) - patch_size // 2
    phases = (-math.pi * distance / patch_size) * (frequency * frequency).astype(jnp.float32)
    return phases[:, None] + phases[None, :]


def forward_fft(field_in):
    return jnp.fft.fft2(field_in, norm="ortho")


def inverse_fft(field_in):
    return jnp.fft.ifft2(field_in, norm="ortho")


def reference(object_slices, probe, positions, counts, measured):
    summed_phase = kernel_phase(PROBE_PATCH_SIDE)
    propagator = jnp.cos(summed_phase) + 1j * jnp.sin(summed_phase)
    probe_field = probe[0] + 1j * probe[1]
    number_of_slots = N_GY * N_GX * P_MAX
    flattened_scan_positions = positions.reshape(number_of_slots, 2).astype(jnp.int32)
    flattened_measurements = measured.reshape(number_of_slots, PROBE_PATCH_SIDE, PROBE_PATCH_SIDE)
    active_slot_mask = (jnp.arange(P_MAX)[None, None, :] < counts[:, :, None]).reshape(number_of_slots).astype(jnp.float32)
    zero_index = jnp.zeros((), jnp.int32)

    def single_patch(carried, scanned):
        loss_gradient, probe_intensity_sum = carried
        corner, observed, weighting = scanned
        start = (zero_index, zero_index, corner[0].astype(jnp.int32), corner[1].astype(jnp.int32))
        window = lax.dynamic_slice(object_slices, start, (SLICES, 2, PROBE_PATCH_SIDE, PROBE_PATCH_SIDE))
        layers = window[:, 0] + 1j * window[:, 1]
        current_wave = probe_field * layers[0]
        arriving = []
        for s in range(1, SLICES):
            propagated = inverse_fft(propagator * forward_fft(current_wave))
            arriving.append(propagated)
            current_wave = propagated * layers[s]
        far_field = forward_fft(current_wave)
        intensity = far_field.real ** 2 + far_field.imag ** 2
        residual = weighting * (intensity - observed)
        backward = inverse_fft(residual * far_field)
        pieces = [None] * SLICES
        for s in range(SLICES - 1, 0, -1):
            pieces[s] = jnp.conj(arriving[s - 1]) * backward
            backward = inverse_fft(jnp.conj(propagator) * forward_fft(jnp.conj(layers[s]) * backward))
        pieces[0] = jnp.conj(probe_field) * backward
        probe_term = jnp.conj(layers[0]) * backward
        stacked = jnp.stack(pieces)
        update = jnp.stack([stacked.real, stacked.imag], axis=1)
        current = lax.dynamic_slice(loss_gradient, start, (SLICES, 2, PROBE_PATCH_SIDE, PROBE_PATCH_SIDE))
        loss_gradient = lax.dynamic_update_slice(loss_gradient, current + update, start)
        probe_intensity_sum = probe_intensity_sum + jnp.stack([probe_term.real, probe_term.imag])
        return (loss_gradient, probe_intensity_sum), None

    starting_guess = (jnp.zeros((SLICES, 2, ROWS, COLS), jnp.float32), jnp.zeros((2, PROBE_PATCH_SIDE, PROBE_PATCH_SIDE), jnp.float32))
    (loss_gradient, probe_intensity_sum), ignored_argument = lax.scan(single_patch, starting_guess, (flattened_scan_positions, flattened_measurements, active_slot_mask))
    return loss_gradient, probe_intensity_sum / jnp.sum(counts).astype(jnp.float32)
```

```python
import math

import jax
import jax.numpy as jnp
import ml_dtypes
import numpy as np
from jax import lax
from jax.experimental import pallas as pl
from jax.experimental.pallas import tpu as pltpu
from jax.sharding import PartitionSpec as P

distance = 0.5
SIDE = 128
HALF = 64
SLICES = 4
SLOTS = 2
RUN = 8
Z_HI, Z_LO, N_X = 4, 4, 4


def split_table(matrix):
    real, imag = matrix.real, matrix.imag
    right = np.block([[real, imag], [-imag, real]]).astype(np.float32)
    parts = []
    for table in (right, right.T):
        high = table.astype(ml_dtypes.bfloat16)
        low = (table - high.astype(np.float32)).astype(ml_dtypes.bfloat16)
        parts.append(np.stack([high, low]))
    return np.stack(parts)


def tables():
    indices = np.arange(SIDE)
    fourier = np.exp(-2j * math.pi / SIDE * (np.outer(indices, indices) % SIDE)) / math.sqrt(SIDE)
    frequency = (indices + SIDE // 2) % SIDE - SIDE // 2
    phase = np.exp(-1j * math.pi * distance / SIDE * frequency * frequency)
    propagator = np.conj(fourier) @ (phase[:, None] * fourier)
    return np.stack([split_table(propagator), split_table(fourier)])


def split_value(value):
    high = value.astype(jnp.bfloat16)
    return high, (value - high.astype(jnp.float32)).astype(jnp.bfloat16)


def two_sided(fields, table_ref, which, conjugate):
    first, second = (1, 0) if conjugate else (0, 1)
    slots = len(fields)
    stacked = jnp.concatenate([jnp.concatenate(pair, axis=1) for pair in fields], axis=0)
    high, low = split_value(stacked)
    w_high, w_low = table_ref[which, first, 0], table_ref[which, first, 1]
    half = jnp.dot(
        jnp.concatenate([high, low, high], axis=1),
        jnp.concatenate([w_high, w_high, w_low], axis=0),
        preferred_element_type=jnp.float32,
    )
    rows = []
    for part in range(2):
        rows.append(
            jnp.concatenate(
                [half[k * SIDE : (k + 1) * SIDE, part * SIDE : (part + 1) * SIDE] for k in range(slots)],
                axis=1,
            )
        )
    high, low = split_value(jnp.concatenate(rows, axis=0))
    w_high, w_low = table_ref[which, second, 0], table_ref[which, second, 1]
    full = jnp.dot(
        jnp.concatenate([w_high, w_high, w_low], axis=1),
        jnp.concatenate([high, low, high], axis=0),
        preferred_element_type=jnp.float32,
    )
    return [
        (full[:SIDE, k * SIDE : (k + 1) * SIDE], full[SIDE:, k * SIDE : (k + 1) * SIDE])
        for k in range(slots)
    ]


def times(a, b):
    return (a[0] * b[0] - a[1] * b[1], a[0] * b[1] + a[1] * b[0])


def conj_times(a, b):
    return (a[0] * b[0] + a[1] * b[1], a[0] * b[1] - a[1] * b[0])


def patch_kernel(
    corner_ref,
    count_ref,
    own_ref,
    edge_up_ref,
    edge_down_ref,
    mid_up_ref,
    mid_down_ref,
    rim_left_ref,
    rim_right_ref,
    probe_ref,
    measured_ref,
    table_ref,
    own_out,
    edge_up_out,
    edge_down_out,
    mid_up_out,
    mid_down_out,
    rim_left_out,
    rim_right_out,
    payload_out,
    extended,
    windows,
    waves,
    total,
):
    low_lanes = lax.broadcasted_iota(jnp.int32, (HALF, SIDE), 1) < HALF
    for s in range(SLICES):
        for c in range(2):
            extended[s, c, 1, HALF : 2 * HALF, :] = own_ref[s, c, :, :SIDE]
            extended[s, c, 2, HALF : 2 * HALF, :] = own_ref[s, c, :, SIDE:]
            for b, edge_ref, mid_ref in ((0, edge_up_ref, mid_up_ref), (2, edge_down_ref, mid_down_ref)):
                edge, mid = edge_ref[s, c], mid_ref[s, c]
                extended[s, c, 1, b * HALF : (b + 1) * HALF, :] = jnp.where(low_lanes, edge, mid)
                extended[s, c, 2, b * HALF : (b + 1) * HALF, :] = jnp.where(low_lanes, mid, edge)
        for b in range(3):
            left, right = rim_left_ref[s, b], rim_right_ref[s, b]
            extended[s, 0, 0, b * HALF : (b + 1) * HALF, :] = pltpu.roll(left, HALF, 1)
            extended[s, 1, 0, b * HALF : (b + 1) * HALF, :] = left
            extended[s, 0, 3, b * HALF : (b + 1) * HALF, :] = right
            extended[s, 1, 3, b * HALF : (b + 1) * HALF, :] = pltpu.roll(right, HALF, 1)

    lanes = lax.broadcasted_iota(jnp.int32, (SIDE, SIDE), 1)
    places = []
    for k in range(SLOTS):
        row, col = corner_ref[k, 0], corner_ref[k, 1] + HALF
        places.append((row, col // SIDE, col % SIDE))
    for k in range(SLOTS):
        row, block, shift = places[k]
        back = (SIDE - shift) % SIDE
        inside = lanes < SIDE - shift
        for s in range(SLICES):
            for c in range(2):
                near = extended[s, c, block, pl.ds(row, SIDE), :]
                far = extended[s, c, block + 1, pl.ds(row, SIDE), :]
                windows[k, s, c] = jnp.where(inside, pltpu.roll(near, back, 1), pltpu.roll(far, back, 1))

    probe = (probe_ref[0], probe_ref[1])

    def layer(k, s):
        return (windows[k, s, 0], windows[k, s, 1])

    slots = range(SLOTS)
    fields = [times(probe, layer(k, 0)) for k in slots]
    for s in range(1, SLICES):
        arrived = two_sided(fields, table_ref, 0, False)
        for k in slots:
            waves[k, s - 1, 0] = arrived[k][0]
            waves[k, s - 1, 1] = arrived[k][1]
        fields = [times(arrived[k], layer(k, s)) for k in slots]
    far_fields = two_sided(fields, table_ref, 1, False)
    scaled = []
    for k in slots:
        real, imag = far_fields[k]
        residual = jnp.where(k < count_ref[0], real * real + imag * imag - measured_ref[k], 0.0)
        scaled.append((residual * real, residual * imag))
    backward = two_sided(scaled, table_ref, 1, True)

    total[...] = jnp.zeros_like(total)

    def add(k, s, pair):
        row, block, shift = places[k]
        inside = lanes >= shift
        for c in range(2):
            moved = pltpu.roll(pair[c], shift, 1)
            total[s, c, block, pl.ds(row, SIDE), :] += jnp.where(inside, moved, 0.0)
            total[s, c, block + 1, pl.ds(row, SIDE), :] += jnp.where(inside, 0.0, moved)

    for s in range(SLICES - 1, 0, -1):
        for k in slots:
            add(k, s, conj_times((waves[k, s - 1, 0], waves[k, s - 1, 1]), backward[k]))
        backward = two_sided([conj_times(layer(k, s), backward[k]) for k in slots], table_ref, 0, True)
    for k in slots:
        add(k, 0, conj_times(probe, backward[k]))
    terms = [conj_times(layer(k, 0), backward[k]) for k in slots]
    for c in range(2):
        summed = (terms[0][c] + terms[1][c]).reshape(16, 8, SIDE)
        payload_out[c * 16 : (c + 1) * 16, 0:8, :] = summed
    payload_out[:, 8:16, :] = jnp.full((32, 8, SIDE), count_ref[0].astype(jnp.float32), jnp.float32)

    for s in range(SLICES):
        for c in range(2):
            own_out[s, c, :, :SIDE] = total[s, c, 1, HALF : 2 * HALF, :]
            own_out[s, c, :, SIDE:] = total[s, c, 2, HALF : 2 * HALF, :]
            for b, edge_out, mid_out in ((0, edge_up_out, mid_up_out), (2, edge_down_out, mid_down_out)):
                first = total[s, c, 1, b * HALF : (b + 1) * HALF, :]
                second = total[s, c, 2, b * HALF : (b + 1) * HALF, :]
                edge_out[s, c] = jnp.where(low_lanes, first, second)
                mid_out[s, c] = jnp.where(low_lanes, second, first)
        for b in range(3):
            rows = slice(b * HALF, (b + 1) * HALF)
            rim_left_out[s, b] = jnp.where(
                low_lanes, pltpu.roll(total[s, 0, 0, rows, :], HALF, 1), total[s, 1, 0, rows, :]
            )
            rim_right_out[s, b] = jnp.where(
                low_lanes, total[s, 0, 3, rows, :], pltpu.roll(total[s, 1, 3, rows, :], HALF, 1)
            )


def gradients(corners, count, own, edge_up, edge_down, mid_up, mid_down, rim_left, rim_right, probe, measured, table):
    f32 = jnp.float32
    band = jax.ShapeDtypeStruct((SLICES, 2, HALF, SIDE), f32)
    rim = jax.ShapeDtypeStruct((SLICES, 3, HALF, SIDE), f32)
    vmem = pl.BlockSpec(memory_space=pltpu.VMEM)
    smem = pl.BlockSpec(memory_space=pltpu.SMEM)
    return pl.pallas_call(
        patch_kernel,
        out_shape=[
            jax.ShapeDtypeStruct((SLICES, 2, HALF, 2 * SIDE), f32),
            band,
            band,
            band,
            band,
            rim,
            rim,
            jax.ShapeDtypeStruct((32, 16, SIDE), f32),
        ],
        in_specs=[smem, smem] + [vmem] * 10,
        out_specs=[vmem] * 8,
        scratch_shapes=[
            pltpu.VMEM((SLICES, 2, 4, 3 * HALF, SIDE), f32),
            pltpu.VMEM((SLOTS, SLICES, 2, SIDE, SIDE), f32),
            pltpu.VMEM((SLOTS, SLICES - 1, 2, SIDE, SIDE), f32),
            pltpu.VMEM((SLICES, 2, 4, 3 * HALF, SIDE), f32),
        ],
        compiler_params=pltpu.CompilerParams(vmem_limit_bytes=40 * 1024 * 1024),
    )(corners, count, own, edge_up, edge_down, mid_up, mid_down, rim_left, rim_right, probe, measured, table)


def pairs(count, step):
    return [(i, step(i)) for i in range(count) if step(i) is not None and 0 <= step(i) < count]


def hop_down(mid, count):
    far = lax.ppermute(mid, "gy", pairs(count, lambda i: i + RUN if i % RUN == RUN - 1 else None))
    here = lax.axis_index("gy") % RUN == RUN - 1
    step = lambda i: i + 1 if i % RUN != RUN - 1 else (i - RUN + 1 if i >= RUN else None)
    return lax.ppermute(jnp.where(here, far, mid), "gy", pairs(count, step))


def hop_up(mid, count):
    far = lax.ppermute(mid, "gy", pairs(count, lambda i: i - RUN if i % RUN == 0 else None))
    here = lax.axis_index("gy") % RUN == 0
    step = lambda i: i - 1 if i % RUN != 0 else (i + RUN - 1 if i < count - RUN else None)
    return lax.ppermute(jnp.where(here, far, mid), "gy", pairs(count, step))


def near_groups():
    return [
        [(x * Z_LO + low) * Z_HI * RUN + high * RUN + m for x in range(N_X) for m in range(RUN)]
        for low in range(Z_LO)
        for high in range(Z_HI)
    ]


def far_groups():
    return [
        [(x * Z_LO + low) * Z_HI * RUN + high * RUN + m for high in range(Z_HI) for low in range(Z_LO)]
        for x in range(N_X)
        for m in range(RUN)
    ]


def exchange(pieces, groups):
    return lax.all_to_all(pieces, ("gx", "gy"), 0, 0, tiled=True, axis_index_groups=groups)


def body(object_slices, probe, positions, counts, measured):
    n_gy, n_gx = lax.axis_size("gy"), lax.axis_size("gx")
    down = pairs(n_gy, lambda i: i + 1)
    up = pairs(n_gy, lambda i: i - 1)
    right = pairs(n_gx, lambda i: i + 1)
    left = pairs(n_gx, lambda i: i - 1)
    cols = object_slices.shape[3]

    mid = jnp.concatenate([object_slices[..., SIDE : SIDE + HALF], object_slices[..., HALF:SIDE]], axis=3)
    edge = jnp.concatenate([object_slices[..., :HALF], object_slices[..., cols - HALF :]], axis=3)
    mid_up = hop_down(mid, n_gy)
    mid_down = hop_up(mid, n_gy)
    edge_up = lax.ppermute(edge, "gy", down)
    edge_down = lax.ppermute(edge, "gy", up)
    bands = jnp.stack([edge_up, edge, edge_down], axis=1)
    lefts = jnp.concatenate([bands[:, :, 0, :, :HALF], bands[:, :, 1, :, :HALF]], axis=3)
    rights = jnp.concatenate([bands[:, :, 0, :, HALF:], bands[:, :, 1, :, HALF:]], axis=3)
    rim_left = lax.ppermute(rights, "gx", right)
    rim_right = lax.ppermute(lefts, "gx", left)

    start = jnp.stack([lax.axis_index("gy") * HALF, lax.axis_index("gx") * cols]).astype(jnp.int32)
    corners = positions[0, 0] - start[None, :] + HALF
    own, edge_up, edge_down, mid_up, mid_down, rim_left, rim_right, payload = gradients(
        corners,
        counts[0],
        object_slices,
        edge_up,
        edge_down,
        mid_up,
        mid_down,
        rim_left,
        rim_right,
        probe,
        measured[0, 0],
        jnp.asarray(tables()),
    )

    from_right = lax.ppermute(rim_left, "gx", left)
    from_left = lax.ppermute(rim_right, "gx", right)
    mid_sum = hop_up(mid_up, n_gy) + hop_down(mid_down, n_gy)

    def rim_bands(b):
        return jnp.stack(
            [
                jnp.concatenate([from_left[:, b, :, :HALF], from_right[:, b, :, :HALF]], axis=2),
                jnp.concatenate([from_left[:, b, :, HALF:], from_right[:, b, :, HALF:]], axis=2),
            ],
            axis=1,
        )

    edge_sum = (
        lax.ppermute(edge_up + rim_bands(0), "gy", up)
        + lax.ppermute(edge_down + rim_bands(2), "gy", down)
        + rim_bands(1)
    )

    near, far = near_groups(), far_groups()
    part = jnp.sum(exchange(payload, near), axis=0)
    part = jnp.sum(exchange(jnp.broadcast_to(part, (Z_LO * Z_HI, 16, SIDE)), far), axis=0)
    part = part[:8] / part[8:]
    probe_grad = exchange(jnp.broadcast_to(part, (32, 8, SIDE)), near).reshape(2, SIDE, SIDE)

    object_grad = own + jnp.concatenate(
        [edge_sum[..., :HALF], mid_sum[..., HALF:], mid_sum[..., :HALF], edge_sum[..., HALF:]], axis=3
    )
    return object_grad, probe_grad


def solution(mesh):
    placed = (
        P(None, None, "gy", "gx"),
        P(),
        P("gy", "gx", None, None),
        P("gy", "gx"),
        P("gy", "gx", None, None, None),
    )
    return jax.shard_map(
        body,
        mesh=mesh,
        in_specs=placed,
        out_specs=(P(None, None, "gy", "gx"), P()),
        check_vma=False,
    )
```

```python
import math

import jax
import jax.numpy as jnp
import ml_dtypes
import numpy as np
from jax import lax
from jax.experimental import pallas as pl
from jax.experimental.layout import Layout, with_layout_constraint
from jax.experimental.pallas import tpu as pltpu
from jax.sharding import PartitionSpec as P

distance = 0.5
SIDE = 128
HALF = 64
SLICES = 4
SLOTS = 2
RUN = 8
Z_HI, Z_LO, N_X = 4, 4, 4
VMEM_BYTES = 32 * 1024 * 1024


def split_table(matrix):
    real, imag = matrix.real, matrix.imag
    right = np.block([[real, imag], [-imag, real]]).astype(np.float32)
    parts = []
    for table in (right, right.T):
        high = table.astype(ml_dtypes.bfloat16)
        low = (table - high.astype(np.float32)).astype(ml_dtypes.bfloat16)
        parts.append(np.stack([high, low]))
    return np.stack(parts)


def tables():
    indices = np.arange(SIDE)
    fourier = np.exp(-2j * math.pi / SIDE * (np.outer(indices, indices) % SIDE)) / math.sqrt(SIDE)
    frequency = (indices + SIDE // 2) % SIDE - SIDE // 2
    phase = np.exp(-1j * math.pi * distance / SIDE * frequency * frequency)
    propagator = np.conj(fourier) @ (phase[:, None] * fourier)
    return np.stack([split_table(propagator), split_table(fourier)])


def split_value(value):
    high = value.astype(jnp.bfloat16)
    return high, (value - high.astype(jnp.float32)).astype(jnp.bfloat16)


def two_sided(fields, table_ref, which, conjugate):
    first, second = (1, 0) if conjugate else (0, 1)
    slots = len(fields)
    stacked = jnp.concatenate([jnp.concatenate(pair, axis=1) for pair in fields], axis=0)
    high, low = split_value(stacked)
    w_high, w_low = table_ref[which, first, 0], table_ref[which, first, 1]
    half = jnp.dot(
        jnp.concatenate([high, low, high], axis=1),
        jnp.concatenate([w_high, w_high, w_low], axis=0),
        preferred_element_type=jnp.float32,
    )
    rows = []
    for part in range(2):
        rows.append(
            jnp.concatenate(
                [half[k * SIDE : (k + 1) * SIDE, part * SIDE : (part + 1) * SIDE] for k in range(slots)],
                axis=1,
            )
        )
    high, low = split_value(jnp.concatenate(rows, axis=0))
    w_high, w_low = table_ref[which, second, 0], table_ref[which, second, 1]
    full = jnp.dot(
        jnp.concatenate([w_high, w_high, w_low], axis=1),
        jnp.concatenate([high, low, high], axis=0),
        preferred_element_type=jnp.float32,
    )
    return [
        (full[:SIDE, k * SIDE : (k + 1) * SIDE], full[SIDE:, k * SIDE : (k + 1) * SIDE])
        for k in range(slots)
    ]


def times(a, b):
    return (a[0] * b[0] - a[1] * b[1], a[0] * b[1] + a[1] * b[0])


def conj_times(a, b):
    return (a[0] * b[0] + a[1] * b[1], a[0] * b[1] - a[1] * b[0])


def patch_kernel(
    corner_ref,
    count_ref,
    odd_ref,
    own_ref,
    chip_ref,
    core_ref,
    chip_one_ref,
    chip_two_ref,
    own_rims_ref,
    core_rims_ref,
    probe_ref,
    measured_ref,
    table_ref,
    own_out,
    edge_out,
    mid_out,
    core_out,
    one_out,
    two_out,
    payload_out,
    extended,
    windows,
    waves,
    total,
):
    low_lanes = lax.broadcasted_iota(jnp.int32, (HALF, SIDE), 1) < HALF
    chip_row = pl.multiple_of(odd_ref[0] * 2 * HALF, HALF)
    core_row = pl.multiple_of((1 - odd_ref[0]) * 2 * HALF, HALF)
    bands = (pl.ds(chip_row, HALF), slice(HALF, 2 * HALF), pl.ds(core_row, HALF))
    odd_column = odd_ref[1] == 1
    for s in range(SLICES):
        for c in range(2):
            for b, band_ref in enumerate((chip_ref, own_ref, core_ref)):
                extended[s, c, 1, bands[b], :] = band_ref[s, c, :, :SIDE]
                extended[s, c, 2, bands[b], :] = band_ref[s, c, :, SIDE:]
        rims = (
            (chip_one_ref[s], chip_two_ref[s]),
            (own_rims_ref[0, s], own_rims_ref[1, s]),
            (core_rims_ref[0, s], core_rims_ref[1, s]),
        )
        for b, (one, two) in enumerate(rims):
            left = jnp.where(odd_column, two, one)
            right = jnp.where(odd_column, one, two)
            extended[s, 0, 0, bands[b], :] = pltpu.roll(left, HALF, 1)
            extended[s, 1, 0, bands[b], :] = left
            extended[s, 0, 3, bands[b], :] = right
            extended[s, 1, 3, bands[b], :] = pltpu.roll(right, HALF, 1)

    lanes = lax.broadcasted_iota(jnp.int32, (SIDE, SIDE), 1)
    places = []
    for k in range(SLOTS):
        row, col = corner_ref[k, 0], corner_ref[k, 1] + HALF
        places.append((row, col // SIDE, col % SIDE))
    for k in range(SLOTS):
        row, block, shift = places[k]
        back = (SIDE - shift) % SIDE
        inside = lanes < SIDE - shift
        for s in range(SLICES):
            for c in range(2):
                near = extended[s, c, block, pl.ds(row, SIDE), :]
                far = extended[s, c, block + 1, pl.ds(row, SIDE), :]
                windows[k, s, c] = jnp.where(inside, pltpu.roll(near, back, 1), pltpu.roll(far, back, 1))

    probe = (probe_ref[0], probe_ref[1])

    def layer(k, s):
        return (windows[k, s, 0], windows[k, s, 1])

    slots = range(SLOTS)
    fields = [times(probe, layer(k, 0)) for k in slots]
    for s in range(1, SLICES):
        arrived = two_sided(fields, table_ref, 0, False)
        for k in slots:
            waves[k, s - 1, 0] = arrived[k][0]
            waves[k, s - 1, 1] = arrived[k][1]
        fields = [times(arrived[k], layer(k, s)) for k in slots]
    far_fields = two_sided(fields, table_ref, 1, False)
    scaled = []
    for k in slots:
        real, imag = far_fields[k]
        residual = jnp.where(k < count_ref[0], real * real + imag * imag - measured_ref[k], 0.0)
        scaled.append((residual * real, residual * imag))
    backward = two_sided(scaled, table_ref, 1, True)

    total[...] = jnp.zeros_like(total)

    def add(k, s, pair):
        row, block, shift = places[k]
        inside = lanes >= shift
        for c in range(2):
            moved = pltpu.roll(pair[c], shift, 1)
            total[s, c, block, pl.ds(row, SIDE), :] += jnp.where(inside, moved, 0.0)
            total[s, c, block + 1, pl.ds(row, SIDE), :] += jnp.where(inside, 0.0, moved)

    for s in range(SLICES - 1, 0, -1):
        for k in slots:
            add(k, s, conj_times((waves[k, s - 1, 0], waves[k, s - 1, 1]), backward[k]))
        backward = two_sided([conj_times(layer(k, s), backward[k]) for k in slots], table_ref, 0, True)
    for k in slots:
        add(k, 0, conj_times(probe, backward[k]))
    terms = [conj_times(layer(k, 0), backward[k]) for k in slots]
    for c in range(2):
        summed = (terms[0][c] + terms[1][c]).reshape(16, 8, SIDE)
        payload_out[c * 16 : (c + 1) * 16, 0:8, :] = summed
    payload_out[:, 8:16, :] = jnp.full((32, 8, SIDE), count_ref[0].astype(jnp.float32), jnp.float32)

    for s in range(SLICES):
        for c in range(2):
            first, second = total[s, c, 1, bands[0], :], total[s, c, 2, bands[0], :]
            edge_out[s, c] = jnp.where(low_lanes, first, second)
            mid_out[s, c] = jnp.where(low_lanes, second, first)
            for b, band_out in ((1, own_out), (2, core_out)):
                band_out[s, c, :, :SIDE] = total[s, c, 1, bands[b], :]
                band_out[s, c, :, SIDE:] = total[s, c, 2, bands[b], :]
        for b in range(3):
            left = jnp.where(
                low_lanes, pltpu.roll(total[s, 0, 0, bands[b], :], HALF, 1), total[s, 1, 0, bands[b], :]
            )
            right = jnp.where(
                low_lanes, total[s, 0, 3, bands[b], :], pltpu.roll(total[s, 1, 3, bands[b], :], HALF, 1)
            )
            one_out[s, b] = jnp.where(odd_column, right, left)
            two_out[s, b] = jnp.where(odd_column, left, right)


def gradients(*operands):
    f32 = jnp.float32
    rim = jax.ShapeDtypeStruct((SLICES, 3, HALF, SIDE), f32)

    def band(width):
        return jax.ShapeDtypeStruct((SLICES, 2, HALF, width), f32)

    shapes = [
        band(2 * SIDE),
        band(SIDE),
        band(SIDE),
        band(2 * SIDE),
        rim,
        rim,
        jax.ShapeDtypeStruct((32, 16, SIDE), f32),
    ]

    def whole(array):
        return pl.BlockSpec(array.shape, lambda i, zeros=(0,) * len(array.shape): zeros)

    smem = pl.BlockSpec(memory_space=pltpu.SMEM)
    return pl.pallas_call(
        patch_kernel,
        grid=(1,),
        out_shape=shapes,
        in_specs=[smem] * 3 + [whole(array) for array in operands[3:]],
        out_specs=[whole(array) for array in shapes],
        scratch_shapes=[
            pltpu.VMEM((SLICES, 2, 4, 3 * HALF, SIDE), f32),
            pltpu.VMEM((SLOTS, SLICES, 2, SIDE, SIDE), f32),
            pltpu.VMEM((SLOTS, SLICES - 1, 2, SIDE, SIDE), f32),
            pltpu.VMEM((SLICES, 2, 4, 3 * HALF, SIDE), f32),
        ],
        compiler_params=pltpu.CompilerParams(vmem_limit_bytes=VMEM_BYTES),
    )(*operands)


def pack(field):
    return jnp.concatenate([field[:, 0], field[:, 1]], axis=-1)


def unpack(field):
    return jnp.stack([field[..., :HALF], field[..., HALF:]], axis=1)


def near_groups():
    return [
        [(x * Z_LO + low) * Z_HI * RUN + high * RUN + m for x in range(N_X) for m in range(RUN)]
        for low in range(Z_LO)
        for high in range(Z_HI)
    ]


def far_groups():
    return [
        [(x * Z_LO + low) * Z_HI * RUN + high * RUN + m for high in range(Z_HI) for low in range(Z_LO)]
        for x in range(N_X)
        for m in range(RUN)
    ]


def exchange(pieces, groups):
    return lax.all_to_all(pieces, ("gx", "gy"), 0, 0, tiled=True, axis_index_groups=groups)


def plain(array):
    return with_layout_constraint(array, Layout(major_to_minor=tuple(range(array.ndim))))


def partners(axis, first):
    count = lax.axis_size(axis)
    both = [(i, i + 1) for i in range(first, count - 1, 2)]
    return both + [(j, i) for i, j in both]


def body(object_slices, probe, positions, counts, measured):
    cols = object_slices.shape[3]
    row, col = lax.axis_index("gy"), lax.axis_index("gx")
    odd_column = col % 2 == 1
    chips, cores = partners("gy", 1), partners("gy", 0)
    ones, twos = partners("gx", 1), partners("gx", 0)
    rows = lax.axis_size("gy")
    hops = [(i, i + RUN) for i in range(RUN - 1, rows - RUN, RUN)] + [(i, i - RUN) for i in range(RUN, rows, RUN)]
    turns = [(i, j) for i, j in chips if i // RUN == j // RUN]
    turns += [(i + RUN - 1, i) for i in range(RUN, rows, RUN)] + [(i, i + RUN - 1) for i in range(0, rows - RUN, RUN)]
    odd = jnp.stack([row % 2, col % 2]).astype(jnp.int32)

    def swap(first, second):
        return lax.ppermute(first, "gx", ones), lax.ppermute(second, "gx", twos)

    def sides(band):
        left, right = pack(band[..., :HALF]), pack(band[..., cols - HALF :])
        return jnp.where(odd_column, right, left), jnp.where(odd_column, left, right)

    chip_band = plain(lax.ppermute(plain(object_slices), "gy", chips))
    core_band = plain(lax.ppermute(plain(object_slices), "gy", cores))
    own_rims = jnp.stack(swap(*sides(object_slices)))
    corners = positions[0, 0] - jnp.stack([row * HALF, col * cols]).astype(jnp.int32)[None, :] + HALF
    chip_band, own_rims, corners, odd = lax.optimization_barrier((chip_band, own_rims, corners, odd))
    core_rims = lax.ppermute(own_rims, "gy", cores)
    chip_one, chip_two = swap(*sides(chip_band))

    own, edge, mid, to_core, one, two, payload = gradients(
        corners,
        counts[0],
        odd,
        object_slices,
        chip_band,
        core_band,
        chip_one,
        chip_two,
        own_rims,
        core_rims,
        probe,
        measured[0, 0],
        jnp.asarray(tables()),
    )

    def columns(one, two):
        return unpack(jnp.where(odd_column, two, one)), unpack(jnp.where(odd_column, one, two))

    def with_rims(band, one, two):
        left, right = columns(one, two)
        middle = jnp.zeros(band.shape[:3] + (cols - 2 * HALF,), band.dtype)
        return band + jnp.concatenate([left, middle, right], axis=3)

    near, far = near_groups(), far_groups()
    at_end = (row % RUN == 0) | (row % RUN == RUN - 1)
    far_mid = plain(lax.ppermute(plain(mid), "gy", hops))
    mid = plain(lax.ppermute(plain(jnp.where(at_end, far_mid, mid)), "gy", turns))
    one, two = swap(plain(one), plain(two))
    one, two = plain(one), plain(two)
    part = jnp.sum(exchange(payload, near), axis=0)
    edge = edge + jnp.concatenate(columns(one[:, 0], two[:, 0]), axis=3)
    to_core = with_rims(to_core, one[:, 2], two[:, 2])
    edge = plain(lax.ppermute(plain(edge), "gy", chips))
    part = jnp.sum(exchange(jnp.broadcast_to(part, (Z_LO * Z_HI, 16, SIDE)), far), axis=0)
    part = part[:8] / part[8:]
    from_core = plain(lax.ppermute(plain(to_core), "gy", cores))
    probe_grad = exchange(jnp.broadcast_to(part, (32, 8, SIDE)), near).reshape(2, SIDE, SIDE)
    from_chip = jnp.concatenate([edge[..., :HALF], mid[..., HALF:], mid[..., :HALF], edge[..., HALF:]], axis=3)
    return plain(with_rims(own, one[:, 1], two[:, 1]) + from_core + from_chip), probe_grad


def solution(mesh):
    placed = (
        P(None, None, "gy", "gx"),
        P(),
        P("gy", "gx", None, None),
        P("gy", "gx"),
        P("gy", "gx", None, None, None),
    )
    return jax.shard_map(
        body,
        mesh=mesh,
        in_specs=placed,
        out_specs=(P(None, None, "gy", "gx"), P()),
        check_vma=False,
    )
```

```python
import math

import jax
import jax.numpy as jnp
import ml_dtypes
import numpy as np
from jax import lax
from jax.experimental import pallas as pl
from jax.experimental.layout import Layout, with_layout_constraint
from jax.experimental.pallas import tpu as pltpu
from jax.sharding import PartitionSpec as P

distance = 0.5
SIDE = 128
HALF = 64
SLICES = 4
SLOTS = 2
RUN = 8
Z_HI, Z_LO, N_X = 4, 4, 4
VMEM_BYTES = 32 * 1024 * 1024


def split_table(matrix):
    real, imag = matrix.real, matrix.imag
    right = np.block([[real, imag], [-imag, real]]).astype(np.float32)
    parts = []
    for table in (right, right.T):
        high = table.astype(ml_dtypes.bfloat16)
        low = (table - high.astype(np.float32)).astype(ml_dtypes.bfloat16)
        parts.append(np.stack([high, low]))
    return np.stack(parts)


def tables():
    indices = np.arange(SIDE)
    fourier = np.exp(-2j * math.pi / SIDE * (np.outer(indices, indices) % SIDE)) / math.sqrt(SIDE)
    frequency = (indices + SIDE // 2) % SIDE - SIDE // 2
    phase = np.exp(-1j * math.pi * distance / SIDE * frequency * frequency)
    propagator = np.conj(fourier) @ (phase[:, None] * fourier)
    return np.stack([split_table(propagator), split_table(fourier)])


def split_value(value):
    high = value.astype(jnp.bfloat16)
    return high, (value - high.astype(jnp.float32)).astype(jnp.bfloat16)


def two_sided(fields, table_ref, which, conjugate):
    first, second = (1, 0) if conjugate else (0, 1)
    slots = len(fields)
    stacked = jnp.concatenate([jnp.concatenate(pair, axis=1) for pair in fields], axis=0)
    high, low = split_value(stacked)
    w_high, w_low = table_ref[which, first, 0], table_ref[which, first, 1]
    half = jnp.dot(
        jnp.concatenate([high, low, high], axis=1),
        jnp.concatenate([w_high, w_high, w_low], axis=0),
        preferred_element_type=jnp.float32,
    )
    rows = []
    for part in range(2):
        rows.append(
            jnp.concatenate(
                [half[k * SIDE : (k + 1) * SIDE, part * SIDE : (part + 1) * SIDE] for k in range(slots)],
                axis=1,
            )
        )
    high, low = split_value(jnp.concatenate(rows, axis=0))
    w_high, w_low = table_ref[which, second, 0], table_ref[which, second, 1]
    full = jnp.dot(
        jnp.concatenate([w_high, w_high, w_low], axis=1),
        jnp.concatenate([high, low, high], axis=0),
        preferred_element_type=jnp.float32,
    )
    return [
        (full[:SIDE, k * SIDE : (k + 1) * SIDE], full[SIDE:, k * SIDE : (k + 1) * SIDE])
        for k in range(slots)
    ]


def times(a, b):
    return (a[0] * b[0] - a[1] * b[1], a[0] * b[1] + a[1] * b[0])


def conj_times(a, b):
    return (a[0] * b[0] + a[1] * b[1], a[0] * b[1] - a[1] * b[0])


def patch_kernel(
    corner_ref,
    count_ref,
    odd_ref,
    own_ref,
    chip_ref,
    core_ref,
    chip_one_ref,
    chip_two_ref,
    own_rims_ref,
    core_rims_ref,
    probe_ref,
    measured_ref,
    table_ref,
    own_out,
    edge_out,
    mid_out,
    core_out,
    one_out,
    two_out,
    payload_out,
    extended,
    windows,
    waves,
    total,
):
    low_lanes = lax.broadcasted_iota(jnp.int32, (HALF, SIDE), 1) < HALF
    chip_row = pl.multiple_of(odd_ref[0] * 2 * HALF, HALF)
    core_row = pl.multiple_of((1 - odd_ref[0]) * 2 * HALF, HALF)
    bands = (pl.ds(chip_row, HALF), slice(HALF, 2 * HALF), pl.ds(core_row, HALF))
    odd_column = odd_ref[1] == 1
    for s in range(SLICES):
        for c in range(2):
            for b, band_ref in enumerate((chip_ref, own_ref, core_ref)):
                extended[s, c, 1, bands[b], :] = band_ref[s, c, :, :SIDE]
                extended[s, c, 2, bands[b], :] = band_ref[s, c, :, SIDE:]
        rims = (
            (chip_one_ref[s], chip_two_ref[s]),
            (own_rims_ref[0, s], own_rims_ref[1, s]),
            (core_rims_ref[0, s], core_rims_ref[1, s]),
        )
        for b, (one, two) in enumerate(rims):
            left = jnp.where(odd_column, two, one)
            right = jnp.where(odd_column, one, two)
            extended[s, 0, 0, bands[b], :] = pltpu.roll(left, HALF, 1)
            extended[s, 1, 0, bands[b], :] = left
            extended[s, 0, 3, bands[b], :] = right
            extended[s, 1, 3, bands[b], :] = pltpu.roll(right, HALF, 1)

    lanes = lax.broadcasted_iota(jnp.int32, (SIDE, SIDE), 1)
    places = []
    for k in range(SLOTS):
        row, col = corner_ref[k, 0], corner_ref[k, 1] + HALF
        places.append((row, col // SIDE, col % SIDE))
    for k in range(SLOTS):
        row, block, shift = places[k]
        back = (SIDE - shift) % SIDE
        inside = lanes < SIDE - shift
        for s in range(SLICES):
            for c in range(2):
                near = extended[s, c, block, pl.ds(row, SIDE), :]
                far = extended[s, c, block + 1, pl.ds(row, SIDE), :]
                windows[k, s, c] = jnp.where(inside, pltpu.roll(near, back, 1), pltpu.roll(far, back, 1))

    probe = (probe_ref[0], probe_ref[1])

    def layer(k, s):
        return (windows[k, s, 0], windows[k, s, 1])

    slots = range(SLOTS)
    fields = [times(probe, layer(k, 0)) for k in slots]
    for s in range(1, SLICES):
        arrived = two_sided(fields, table_ref, 0, False)
        for k in slots:
            waves[k, s - 1, 0] = arrived[k][0]
            waves[k, s - 1, 1] = arrived[k][1]
        fields = [times(arrived[k], layer(k, s)) for k in slots]
    far_fields = two_sided(fields, table_ref, 1, False)
    scaled = []
    for k in slots:
        real, imag = far_fields[k]
        residual = jnp.where(k < count_ref[0], real * real + imag * imag - measured_ref[k], 0.0)
        scaled.append((residual * real, residual * imag))
    backward = two_sided(scaled, table_ref, 1, True)

    total[...] = jnp.zeros_like(total)

    def add(k, s, pair):
        row, block, shift = places[k]
        inside = lanes >= shift
        for c in range(2):
            moved = pltpu.roll(pair[c], shift, 1)
            total[s, c, block, pl.ds(row, SIDE), :] += jnp.where(inside, moved, 0.0)
            total[s, c, block + 1, pl.ds(row, SIDE), :] += jnp.where(inside, 0.0, moved)

    for s in range(SLICES - 1, 0, -1):
        for k in slots:
            add(k, s, conj_times((waves[k, s - 1, 0], waves[k, s - 1, 1]), backward[k]))
        backward = two_sided([conj_times(layer(k, s), backward[k]) for k in slots], table_ref, 0, True)
    for k in slots:
        add(k, 0, conj_times(probe, backward[k]))
    terms = [conj_times(layer(k, 0), backward[k]) for k in slots]
    for c in range(2):
        summed = (terms[0][c] + terms[1][c]).reshape(16, 8, SIDE)
        payload_out[c * 16 : (c + 1) * 16, 0:8, :] = summed
    payload_out[:, 8:16, :] = jnp.full((32, 8, SIDE), count_ref[0].astype(jnp.float32), jnp.float32)

    for s in range(SLICES):
        for c in range(2):
            first, second = total[s, c, 1, bands[0], :], total[s, c, 2, bands[0], :]
            edge_out[s, c] = jnp.where(low_lanes, first, second)
            mid_out[s, c] = jnp.where(low_lanes, second, first)
            for b, band_out in ((1, own_out), (2, core_out)):
                band_out[s, c, :, :SIDE] = total[s, c, 1, bands[b], :]
                band_out[s, c, :, SIDE:] = total[s, c, 2, bands[b], :]
        for b in range(3):
            left = jnp.where(
                low_lanes, pltpu.roll(total[s, 0, 0, bands[b], :], HALF, 1), total[s, 1, 0, bands[b], :]
            )
            right = jnp.where(
                low_lanes, total[s, 0, 3, bands[b], :], pltpu.roll(total[s, 1, 3, bands[b], :], HALF, 1)
            )
            one_out[s, b] = jnp.where(odd_column, right, left)
            two_out[s, b] = jnp.where(odd_column, left, right)


def gradients(*operands):
    f32 = jnp.float32
    rim = jax.ShapeDtypeStruct((SLICES, 3, HALF, SIDE), f32)

    def band(width):
        return jax.ShapeDtypeStruct((SLICES, 2, HALF, width), f32)

    shapes = [
        band(2 * SIDE),
        band(SIDE),
        band(SIDE),
        band(2 * SIDE),
        rim,
        rim,
        jax.ShapeDtypeStruct((32, 16, SIDE), f32),
    ]

    def whole(array):
        return pl.BlockSpec(array.shape, lambda i, zeros=(0,) * len(array.shape): zeros)

    smem = pl.BlockSpec(memory_space=pltpu.SMEM)
    return pl.pallas_call(
        patch_kernel,
        grid=(1,),
        out_shape=shapes,
        in_specs=[smem] * 3 + [whole(array) for array in operands[3:]],
        out_specs=[whole(array) for array in shapes],
        scratch_shapes=[
            pltpu.VMEM((SLICES, 2, 4, 3 * HALF, SIDE), f32),
            pltpu.VMEM((SLOTS, SLICES, 2, SIDE, SIDE), f32),
            pltpu.VMEM((SLOTS, SLICES - 1, 2, SIDE, SIDE), f32),
            pltpu.VMEM((SLICES, 2, 4, 3 * HALF, SIDE), f32),
        ],
        compiler_params=pltpu.CompilerParams(vmem_limit_bytes=VMEM_BYTES),
    )(*operands)


def pack(field):
    return jnp.concatenate([field[:, 0], field[:, 1]], axis=-1)


def unpack(field):
    return jnp.stack([field[..., :HALF], field[..., HALF:]], axis=1)


def near_groups():
    return [
        [(x * Z_LO + low) * Z_HI * RUN + high * RUN + m for x in range(N_X) for m in range(RUN)]
        for low in range(Z_LO)
        for high in range(Z_HI)
    ]


def far_groups():
    return [
        [(x * Z_LO + low) * Z_HI * RUN + high * RUN + m for high in range(Z_HI) for low in range(Z_LO)]
        for x in range(N_X)
        for m in range(RUN)
    ]


def exchange(pieces, groups):
    return lax.all_to_all(pieces, ("gx", "gy"), 0, 0, tiled=True, axis_index_groups=groups)


def plain(array):
    return with_layout_constraint(array, Layout(major_to_minor=tuple(range(array.ndim))))


def partners(axis, first):
    count = lax.axis_size(axis)
    both = [(i, i + 1) for i in range(first, count - 1, 2)]
    return both + [(j, i) for i, j in both]


def body(object_slices, probe, positions, counts, measured):
    cols = object_slices.shape[3]
    row, col = lax.axis_index("gy"), lax.axis_index("gx")
    odd_column = col % 2 == 1
    chips, cores = partners("gy", 1), partners("gy", 0)
    ones, twos = partners("gx", 1), partners("gx", 0)
    rows = lax.axis_size("gy")
    hops = [(i, i + RUN) for i in range(RUN - 1, rows - RUN, RUN)] + [(i, i - RUN) for i in range(RUN, rows, RUN)]
    turns = [(i, j) for i, j in chips if i // RUN == j // RUN]
    turns += [(i + RUN - 1, i) for i in range(RUN, rows, RUN)] + [(i, i + RUN - 1) for i in range(0, rows - RUN, RUN)]
    odd = jnp.stack([row % 2, col % 2]).astype(jnp.int32)

    def swap(first, second):
        return lax.ppermute(first, "gx", ones), lax.ppermute(second, "gx", twos)

    def sides(band):
        left, right = pack(band[..., :HALF]), pack(band[..., cols - HALF :])
        return jnp.where(odd_column, right, left), jnp.where(odd_column, left, right)

    chip_band = plain(lax.ppermute(plain(object_slices), "gy", chips))
    core_band = plain(lax.ppermute(plain(object_slices), "gy", cores))
    own_rims = jnp.stack(swap(*sides(object_slices)))
    corners = positions[0, 0] - jnp.stack([row * HALF, col * cols]).astype(jnp.int32)[None, :] + HALF
    core_rims = plain(lax.ppermute(plain(own_rims), "gy", cores))
    chip_band, own_rims, corners, odd = lax.optimization_barrier((chip_band, own_rims, corners, odd))
    chip_one, chip_two = swap(*sides(chip_band))

    own, edge, mid, to_core, one, two, payload = gradients(
        corners,
        counts[0],
        odd,
        object_slices,
        chip_band,
        core_band,
        chip_one,
        chip_two,
        own_rims,
        core_rims,
        probe,
        measured[0, 0],
        jnp.asarray(tables()),
    )

    def columns(one, two):
        return unpack(jnp.where(odd_column, two, one)), unpack(jnp.where(odd_column, one, two))

    def with_rims(band, one, two):
        left, right = columns(one, two)
        middle = jnp.zeros(band.shape[:3] + (cols - 2 * HALF,), band.dtype)
        return band + jnp.concatenate([left, middle, right], axis=3)

    near, far = near_groups(), far_groups()
    at_end = (row % RUN == 0) | (row % RUN == RUN - 1)
    far_mid = plain(lax.ppermute(plain(mid), "gy", hops))
    mid = plain(lax.ppermute(plain(jnp.where(at_end, far_mid, mid)), "gy", turns))
    one, two = swap(plain(one), plain(two))
    one, two = plain(one), plain(two)
    part = jnp.sum(exchange(payload, near), axis=0)
    edge = edge + jnp.concatenate(columns(one[:, 0], two[:, 0]), axis=3)
    to_core = with_rims(to_core, one[:, 2], two[:, 2])
    edge = plain(lax.ppermute(plain(edge), "gy", chips))
    part = jnp.sum(exchange(jnp.broadcast_to(part, (Z_LO * Z_HI, 16, SIDE)), far), axis=0)
    part = part[:8] / part[8:]
    from_core = plain(lax.ppermute(plain(to_core), "gy", cores))
    probe_grad = exchange(jnp.broadcast_to(part, (32, 8, SIDE)), near).reshape(2, SIDE, SIDE)
    from_chip = jnp.concatenate([edge[..., :HALF], mid[..., HALF:], mid[..., :HALF], edge[..., HALF:]], axis=3)
    return plain(with_rims(own, one[:, 1], two[:, 1]) + from_core + from_chip), probe_grad


def solution(mesh):
    placed = (
        P(None, None, "gy", "gx"),
        P(),
        P("gy", "gx", None, None),
        P("gy", "gx"),
        P("gy", "gx", None, None, None),
    )
    return jax.shard_map(
        body,
        mesh=mesh,
        in_specs=placed,
        out_specs=(P(None, None, "gy", "gx"), P()),
        check_vma=False,
    )
```

```python
import math

import jax
import jax.numpy as jnp
import ml_dtypes
import numpy as np
from jax import lax
from jax.experimental import pallas as pl
from jax.experimental.layout import Layout, with_layout_constraint
from jax.experimental.pallas import tpu as pltpu
from jax.sharding import PartitionSpec as P

distance = 0.5
SIDE = 128
HALF = 64
SLICES = 4
SLOTS = 2
RUN = 8
Z_HI, Z_LO, N_X = 4, 4, 4
VMEM_BYTES = 32 * 1024 * 1024


def split_table(matrix):
    real, imag = matrix.real, matrix.imag
    right = np.block([[real, imag], [-imag, real]]).astype(np.float32)
    parts = []
    for table in (right, right.T):
        high = table.astype(ml_dtypes.bfloat16)
        low = (table - high.astype(np.float32)).astype(ml_dtypes.bfloat16)
        parts.append(np.stack([high, low]))
    return np.stack(parts)


def tables():
    indices = np.arange(SIDE)
    fourier = np.exp(-2j * math.pi / SIDE * (np.outer(indices, indices) % SIDE)) / math.sqrt(SIDE)
    frequency = (indices + SIDE // 2) % SIDE - SIDE // 2
    phase = np.exp(-1j * math.pi * distance / SIDE * frequency * frequency)
    propagator = np.conj(fourier) @ (phase[:, None] * fourier)
    return np.stack([split_table(propagator), split_table(fourier)])


def split_value(value):
    high = value.astype(jnp.bfloat16)
    return high, (value - high.astype(jnp.float32)).astype(jnp.bfloat16)


def two_sided(fields, table_ref, which, conjugate):
    first, second = (1, 0) if conjugate else (0, 1)
    slots = len(fields)
    stacked = jnp.concatenate([jnp.concatenate(pair, axis=1) for pair in fields], axis=0)
    high, low = split_value(stacked)
    w_high, w_low = table_ref[which, first, 0], table_ref[which, first, 1]
    half = jnp.dot(
        jnp.concatenate([high, low, high], axis=1),
        jnp.concatenate([w_high, w_high, w_low], axis=0),
        preferred_element_type=jnp.float32,
    )
    rows = []
    for part in range(2):
        rows.append(
            jnp.concatenate(
                [half[k * SIDE : (k + 1) * SIDE, part * SIDE : (part + 1) * SIDE] for k in range(slots)],
                axis=1,
            )
        )
    high, low = split_value(jnp.concatenate(rows, axis=0))
    w_high, w_low = table_ref[which, second, 0], table_ref[which, second, 1]
    full = jnp.dot(
        jnp.concatenate([w_high, w_high, w_low], axis=1),
        jnp.concatenate([high, low, high], axis=0),
        preferred_element_type=jnp.float32,
    )
    return [
        (full[:SIDE, k * SIDE : (k + 1) * SIDE], full[SIDE:, k * SIDE : (k + 1) * SIDE])
        for k in range(slots)
    ]


def times(a, b):
    return (a[0] * b[0] - a[1] * b[1], a[0] * b[1] + a[1] * b[0])


def conj_times(a, b):
    return (a[0] * b[0] + a[1] * b[1], a[0] * b[1] - a[1] * b[0])


def patch_kernel(
    corner_ref,
    count_ref,
    odd_ref,
    own_ref,
    chip_ref,
    core_ref,
    chip_one_ref,
    chip_two_ref,
    own_rims_ref,
    core_rims_ref,
    probe_ref,
    measured_ref,
    table_ref,
    own_out,
    edge_out,
    mid_out,
    core_out,
    one_out,
    two_out,
    payload_out,
    extended,
    windows,
    waves,
    total,
):
    low_lanes = lax.broadcasted_iota(jnp.int32, (HALF, SIDE), 1) < HALF
    chip_row = pl.multiple_of(odd_ref[0] * 2 * HALF, HALF)
    core_row = pl.multiple_of((1 - odd_ref[0]) * 2 * HALF, HALF)
    bands = (pl.ds(chip_row, HALF), slice(HALF, 2 * HALF), pl.ds(core_row, HALF))
    odd_column = odd_ref[1] == 1
    def assemble(s):
        for c in range(2):
            for b, band_ref in enumerate((chip_ref, own_ref, core_ref)):
                extended[s, c, 1, bands[b], :] = band_ref[s, c, :, :SIDE]
                extended[s, c, 2, bands[b], :] = band_ref[s, c, :, SIDE:]
        rims = (
            (chip_one_ref[s], chip_two_ref[s]),
            (own_rims_ref[0, s], own_rims_ref[1, s]),
            (core_rims_ref[0, s], core_rims_ref[1, s]),
        )
        for b, (one, two) in enumerate(rims):
            left = jnp.where(odd_column, two, one)
            right = jnp.where(odd_column, one, two)
            extended[s, 0, 0, bands[b], :] = pltpu.roll(left, HALF, 1)
            extended[s, 1, 0, bands[b], :] = left
            extended[s, 0, 3, bands[b], :] = right
            extended[s, 1, 3, bands[b], :] = pltpu.roll(right, HALF, 1)

    lanes = lax.broadcasted_iota(jnp.int32, (SIDE, SIDE), 1)
    places = []
    for k in range(SLOTS):
        row, col = corner_ref[k, 0], corner_ref[k, 1] + HALF
        places.append((row, col // SIDE, col % SIDE))
    def extract(s):
        assemble(s)
        for k in range(SLOTS):
            row, block, shift = places[k]
            back = (SIDE - shift) % SIDE
            inside = lanes < SIDE - shift
            for c in range(2):
                near = extended[s, c, block, pl.ds(row, SIDE), :]
                far = extended[s, c, block + 1, pl.ds(row, SIDE), :]
                windows[k, s, c] = jnp.where(inside, pltpu.roll(near, back, 1), pltpu.roll(far, back, 1))

    probe = (probe_ref[0], probe_ref[1])

    def layer(k, s):
        return (windows[k, s, 0], windows[k, s, 1])

    slots = range(SLOTS)
    extract(0)
    fields = [times(probe, layer(k, 0)) for k in slots]
    for s in range(1, SLICES):
        arrived = two_sided(fields, table_ref, 0, False)
        extract(s)
        for k in slots:
            waves[k, s - 1, 0] = arrived[k][0]
            waves[k, s - 1, 1] = arrived[k][1]
        fields = [times(arrived[k], layer(k, s)) for k in slots]
    far_fields = two_sided(fields, table_ref, 1, False)
    scaled = []
    for k in slots:
        real, imag = far_fields[k]
        residual = jnp.where(k < count_ref[0], real * real + imag * imag - measured_ref[k], 0.0)
        scaled.append((residual * real, residual * imag))
    backward = two_sided(scaled, table_ref, 1, True)

    total[...] = jnp.zeros_like(total)

    def add(k, s, pair):
        row, block, shift = places[k]
        inside = lanes >= shift
        for c in range(2):
            moved = pltpu.roll(pair[c], shift, 1)
            total[s, c, block, pl.ds(row, SIDE), :] += jnp.where(inside, moved, 0.0)
            total[s, c, block + 1, pl.ds(row, SIDE), :] += jnp.where(inside, 0.0, moved)

    def emit(s):
        for c in range(2):
            first, second = total[s, c, 1, bands[0], :], total[s, c, 2, bands[0], :]
            edge_out[s, c] = jnp.where(low_lanes, first, second)
            mid_out[s, c] = jnp.where(low_lanes, second, first)
            for b, band_out in ((1, own_out), (2, core_out)):
                band_out[s, c, :, :SIDE] = total[s, c, 1, bands[b], :]
                band_out[s, c, :, SIDE:] = total[s, c, 2, bands[b], :]
        for b in range(3):
            left = jnp.where(
                low_lanes, pltpu.roll(total[s, 0, 0, bands[b], :], HALF, 1), total[s, 1, 0, bands[b], :]
            )
            right = jnp.where(
                low_lanes, total[s, 0, 3, bands[b], :], pltpu.roll(total[s, 1, 3, bands[b], :], HALF, 1)
            )
            one_out[s, b] = jnp.where(odd_column, right, left)
            two_out[s, b] = jnp.where(odd_column, left, right)

    for s in range(SLICES - 1, 0, -1):
        for k in slots:
            add(k, s, conj_times((waves[k, s - 1, 0], waves[k, s - 1, 1]), backward[k]))
        backward = two_sided([conj_times(layer(k, s), backward[k]) for k in slots], table_ref, 0, True)
        emit(s)
    for k in slots:
        add(k, 0, conj_times(probe, backward[k]))
    emit(0)
    terms = [conj_times(layer(k, 0), backward[k]) for k in slots]
    for c in range(2):
        summed = (terms[0][c] + terms[1][c]).reshape(16, 8, SIDE)
        payload_out[c * 16 : (c + 1) * 16, 0:8, :] = summed
    payload_out[:, 8:16, :] = jnp.full((32, 8, SIDE), count_ref[0].astype(jnp.float32), jnp.float32)


def gradients(*operands):
    f32 = jnp.float32
    rim = jax.ShapeDtypeStruct((SLICES, 3, HALF, SIDE), f32)

    def band(width):
        return jax.ShapeDtypeStruct((SLICES, 2, HALF, width), f32)

    shapes = [
        band(2 * SIDE),
        band(SIDE),
        band(SIDE),
        band(2 * SIDE),
        rim,
        rim,
        jax.ShapeDtypeStruct((32, 16, SIDE), f32),
    ]

    def whole(array):
        return pl.BlockSpec(array.shape, lambda i, zeros=(0,) * len(array.shape): zeros)

    smem = pl.BlockSpec(memory_space=pltpu.SMEM)
    return pl.pallas_call(
        patch_kernel,
        grid=(1,),
        out_shape=shapes,
        in_specs=[smem] * 3 + [whole(array) for array in operands[3:]],
        out_specs=[whole(array) for array in shapes],
        scratch_shapes=[
            pltpu.VMEM((SLICES, 2, 4, 3 * HALF, SIDE), f32),
            pltpu.VMEM((SLOTS, SLICES, 2, SIDE, SIDE), f32),
            pltpu.VMEM((SLOTS, SLICES - 1, 2, SIDE, SIDE), f32),
            pltpu.VMEM((SLICES, 2, 4, 3 * HALF, SIDE), f32),
        ],
        compiler_params=pltpu.CompilerParams(vmem_limit_bytes=VMEM_BYTES),
    )(*operands)


def pack(field):
    return jnp.concatenate([field[:, 0], field[:, 1]], axis=-1)


def unpack(field):
    return jnp.stack([field[..., :HALF], field[..., HALF:]], axis=1)


def near_groups():
    return [
        [(x * Z_LO + low) * Z_HI * RUN + high * RUN + m for x in range(N_X) for m in range(RUN)]
        for low in range(Z_LO)
        for high in range(Z_HI)
    ]


def far_groups():
    return [
        [(x * Z_LO + low) * Z_HI * RUN + high * RUN + m for high in range(Z_HI) for low in range(Z_LO)]
        for x in range(N_X)
        for m in range(RUN)
    ]


def exchange(pieces, groups):
    return lax.all_to_all(pieces, ("gx", "gy"), 0, 0, tiled=True, axis_index_groups=groups)


def plain(array):
    return with_layout_constraint(array, Layout(major_to_minor=tuple(range(array.ndim))))


def partners(axis, first):
    count = lax.axis_size(axis)
    both = [(i, i + 1) for i in range(first, count - 1, 2)]
    return both + [(j, i) for i, j in both]


def body(object_slices, probe, positions, counts, measured):
    cols = object_slices.shape[3]
    row, col = lax.axis_index("gy"), lax.axis_index("gx")
    odd_column = col % 2 == 1
    chips, cores = partners("gy", 1), partners("gy", 0)
    ones, twos = partners("gx", 1), partners("gx", 0)
    rows = lax.axis_size("gy")
    hops = [(i, i + RUN) for i in range(RUN - 1, rows - RUN, RUN)] + [(i, i - RUN) for i in range(RUN, rows, RUN)]
    turns = [(i, j) for i, j in chips if i // RUN == j // RUN]
    turns += [(i + RUN - 1, i) for i in range(RUN, rows, RUN)] + [(i, i + RUN - 1) for i in range(0, rows - RUN, RUN)]
    odd = jnp.stack([row % 2, col % 2]).astype(jnp.int32)

    def swap(first, second):
        return lax.ppermute(first, "gx", ones), lax.ppermute(second, "gx", twos)

    def sides(band):
        left, right = pack(band[..., :HALF]), pack(band[..., cols - HALF :])
        return jnp.where(odd_column, right, left), jnp.where(odd_column, left, right)

    chip_band = plain(lax.ppermute(plain(object_slices), "gy", chips))
    core_band = plain(lax.ppermute(plain(object_slices), "gy", cores))
    own_rims = jnp.stack(swap(*sides(object_slices)))
    corners = positions[0, 0] - jnp.stack([row * HALF, col * cols]).astype(jnp.int32)[None, :] + HALF
    core_rims = plain(lax.ppermute(plain(own_rims), "gy", cores))
    chip_band, own_rims, corners, odd = lax.optimization_barrier((chip_band, own_rims, corners, odd))
    chip_one, chip_two = swap(*sides(chip_band))

    own, edge, mid, to_core, one, two, payload = gradients(
        corners,
        counts[0],
        odd,
        object_slices,
        chip_band,
        core_band,
        chip_one,
        chip_two,
        own_rims,
        core_rims,
        probe,
        measured[0, 0],
        jnp.asarray(tables()),
    )

    def columns(one, two):
        return unpack(jnp.where(odd_column, two, one)), unpack(jnp.where(odd_column, one, two))

    def with_rims(band, one, two):
        left, right = columns(one, two)
        middle = jnp.zeros(band.shape[:3] + (cols - 2 * HALF,), band.dtype)
        return band + jnp.concatenate([left, middle, right], axis=3)

    near, far = near_groups(), far_groups()
    at_end = (row % RUN == 0) | (row % RUN == RUN - 1)
    far_mid = plain(lax.ppermute(plain(mid), "gy", hops))
    mid = plain(lax.ppermute(plain(jnp.where(at_end, far_mid, mid)), "gy", turns))
    one, two = swap(plain(one), plain(two))
    one, two = plain(one), plain(two)
    part = jnp.sum(exchange(payload, near), axis=0)
    edge = edge + jnp.concatenate(columns(one[:, 0], two[:, 0]), axis=3)
    to_core = with_rims(to_core, one[:, 2], two[:, 2])
    edge = plain(lax.ppermute(plain(edge), "gy", chips))
    part = jnp.sum(exchange(jnp.broadcast_to(part, (Z_LO * Z_HI, 16, SIDE)), far), axis=0)
    part = part[:8] / part[8:]
    from_core = plain(lax.ppermute(plain(to_core), "gy", cores))
    probe_grad = exchange(jnp.broadcast_to(part, (32, 8, SIDE)), near).reshape(2, SIDE, SIDE)
    from_chip = jnp.concatenate([edge[..., :HALF], mid[..., HALF:], mid[..., :HALF], edge[..., HALF:]], axis=3)
    return plain(with_rims(own, one[:, 1], two[:, 1]) + from_core + from_chip), probe_grad


def solution(mesh):
    placed = (
        P(None, None, "gy", "gx"),
        P(),
        P("gy", "gx", None, None),
        P("gy", "gx"),
        P("gy", "gx", None, None, None),
    )
    return jax.shard_map(
        body,
        mesh=mesh,
        in_specs=placed,
        out_specs=(P(None, None, "gy", "gx"), P()),
        check_vma=False,
    )
```
